32 devices in a mesh: section: 4 (over y, x), seq: 2 (over core), head: 4 (over z).
Axes of the slice: x: 2, y: 2, z: 4, core: 2. Of those that a mesh axis runs over, the one named last changes fastest.
Arguments:
- encoder_states: bfloat16 [4, 2048, 4096], P(None, 'seq'), may hold values from -6 to 6
- w_kv: bfloat16 [4, 4096, 4096], P(None, None, ('section', 'head')), may hold values from -0.125 to 0.125
- queries: bfloat16 [4, 4, 256, 4, 512], P('section', None, None, None, 'head'), may hold values from -102 to 102
- cotangent: bfloat16 [4, 4, 256, 4, 512], P('section', None, None, None, 'head'), may hold values from -6 to 6
- src_len: int32 [4], replicated, may hold values from 512 to 2048, as said below
- tgt_len: int32 [4], replicated, may hold values from 64 to 256, as said below
Outputs:
- attn_out: bfloat16 [4, 4, 256, 4, 512], P('section', None, 'seq', None, 'head')
- query_grads: bfloat16 [4, 4, 256, 4, 512], P('section', None, 'seq', None, 'head')
- source_grads: bfloat16 [4, 2048, 4096], P(None, 'seq', ('section', 'head'))
The draws below stay inside these ranges and needn't reach their ends.
Inputs may be any that keep to these rules, and one draw needn't show every extreme that they name: `src_len`: at least one sample has all 2048 source tokens. `tgt_len`: at least one sample has all 256 target tokens.
All inputs are finite; a program needn't handle non-finite values.
Results may differ from the reference program's by a relative error of at most 0.014.
The reference program's roundings to bfloat16 on the way (of `key_value`, `probability_low`, `grad_out`, `grad_scores` and `grad_pairs`) count: a program that leaves them out, or rounds other values in their place, can miss the bound.
Values may be sent and summed in bfloat16 or wider, within the bound.
A program may use at most 192 MiB of HBM per device.

```python
import jax
import jax.numpy as jnp
from jax import lax

D = 4096
HD = 128
BATCH = 4
SRC = 2048
TQ = 256
LAYERS = 4
GROUPS = 4
HEAD_COLS = 512
HEADS = 16


def target_lengths(key):
    lengths_drawn = jax.random.randint(key, (BATCH,), TQ // 4, TQ + 1)
    full_row = jax.random.randint(jax.random.fold_in(key, 13), (), 0, BATCH)
    return jnp.where(jnp.arange(BATCH) == full_row, TQ, lengths_drawn).astype(jnp.int32)


def draw_queries(key, part):
    shape = (LAYERS, BATCH, TQ, GROUPS, HEAD_COLS)
    base_key = jax.random.fold_in(key, 3)
    return jnp.clip(jax.random.normal(base_key, shape, jnp.float32), -6.0, 6.0).astype(jnp.bfloat16)


def draw_src_len(key, part):
    lengths_drawn = jax.random.randint(key, (BATCH,), SRC // 4, SRC + 1)
    full_row = jax.random.randint(jax.random.fold_in(key, 11), (), 0, BATCH)
    return jnp.where(jnp.arange(BATCH) == full_row, SRC, lengths_drawn).astype(jnp.int32)


def draw_tgt_len(key, part):
    return target_lengths(key)


def with_spikes(result, stream_key, source, target, parts, factor):
    def block_of(dim):
        return (jnp.arange(result.shape[dim]) // (result.shape[dim] // parts)).reshape((-1,) + (1,) * (result.ndim - 1 - dim))

    first = jax.random.permutation(stream_key, parts)[block_of(target)]
    far = (block_of(target) + parts // 2) % parts
    return jnp.where((block_of(source) == first) | (block_of(source) == far), factor * result, result)


def shard_levels(key, extent, cuts, least, high):
    level = 1.0
    for axis_at, shards_of in cuts:
        steps = jax.random.uniform(jax.random.fold_in(jax.random.fold_in(key, 6), axis_at), (shards_of,), jnp.float32, least / len(cuts), high / len(cuts))
        level = level * jnp.repeat(jnp.exp(steps), extent[axis_at] // shards_of).reshape((-1,) + (1,) * (len(extent) - 1 - axis_at))
    return level


def centred(stream_key, dims, scale, reach, pieces=(), kind=jnp.bfloat16):
    loudness = shard_levels(stream_key, dims, pieces, -0.22, 0.18) if pieces else 1.0
    values = jax.random.normal(stream_key, dims, jnp.float32) * scale * loudness
    return jnp.minimum(jnp.maximum(values, -reach), reach).astype(kind)


def gaussian_with(stream_key, extent, spread, limit, pieces, heavy, kind=jnp.bfloat16):
    drawn = spread * jax.random.normal(stream_key, extent, jnp.float32)
    if pieces:
        drawn = drawn * shard_levels(stream_key, extent, pieces, -0.22, 0.18)
    return jnp.clip(with_spikes(drawn, jax.random.fold_in(stream_key, 3), *heavy), -limit, limit).astype(kind)


def setup_inputs(seed: int = 0) -> dict:
    key_of = jax.random.split(jax.random.key(seed), 7)
    encoder_states = centred(key_of[0], (BATCH, SRC, D), 1.0, 6.0, ((1, 2),))
    w_kv = gaussian_with(key_of[1], (LAYERS, D, HEADS * 2 * HD), D ** -0.5, 0.125, ((2, 16),), (2, 1, 16, 2.0))
    queries = draw_queries(jax.random.fold_in(key_of[6], 71), 0)
    cotangent = centred(key_of[3], (LAYERS, BATCH, TQ, GROUPS, HEAD_COLS), 1.0, 6.0, ((0, 4), (4, 4)))
    src_len = draw_src_len(jax.random.fold_in(key_of[6], 71), 0)
    tgt_len = draw_tgt_len(jax.random.fold_in(key_of[6], 71), 0)
    return {"encoder_states": encoder_states, "w_kv": w_kv, "queries": queries, "cotangent": cotangent, "src_len": src_len, "tgt_len": tgt_len}


masked_score = -1e30


def round_low(value):
    low = value.astype(jnp.bfloat16)
    low = lax.optimization_barrier(low)
    return low.astype(jnp.float32)


def layer_grads(encoder_states, w_layer, query_layer, cot_layer, src_len, tgt_len):
    score_scale = HD ** -0.5
    key_value = jnp.einsum("bsd,dc->bsc", encoder_states.astype(jnp.float32), w_layer.astype(jnp.float32))
    key_value = round_low(key_value).reshape(BATCH, SRC, HEADS, 2, HD)
    key_rows = key_value[:, :, :, 0, :]
    value_rows = key_value[:, :, :, 1, :]
    query_rows = query_layer.astype(jnp.float32).reshape(BATCH, TQ, HEADS, HD)
    scores = jnp.einsum("bthd,bshd->bhts", query_rows, key_rows) * score_scale
    key_live = jnp.arange(SRC, dtype=jnp.int32)[None, :] < src_len[:, None]
    scores = jnp.where(key_live[:, None, None, :], scores, masked_score)
    row_top = jnp.max(scores, axis=-1, keepdims=True)
    exponent = jnp.exp(scores - row_top)
    row_total = jnp.sum(exponent, axis=-1, keepdims=True)
    probability = exponent / row_total
    probability_low = round_low(probability)
    attended = jnp.einsum("bhts,bshd->bthd", probability_low, value_rows)
    out_layer = attended.astype(jnp.bfloat16).reshape(BATCH, TQ, GROUPS, HEAD_COLS)
    query_live = jnp.arange(TQ, dtype=jnp.int32)[None, :] < tgt_len[:, None]
    grad_out = jnp.where(query_live[:, :, None, None], cot_layer.astype(jnp.float32).reshape(BATCH, TQ, HEADS, HD), jnp.float32(0.0))
    row_delta = jnp.transpose(jnp.sum(grad_out * attended, axis=-1), (0, 2, 1))
    grad_probs = jnp.einsum("bthd,bshd->bhts", grad_out, value_rows)
    grad_scores = round_low(probability * (grad_probs - row_delta[..., None]))
    grad_query = (score_scale * jnp.einsum("bhts,bshd->bthd", grad_scores, key_rows)).astype(jnp.bfloat16)
    grad_keys = score_scale * jnp.einsum("bhts,bthd->bshd", grad_scores, query_rows)
    grad_values = jnp.einsum("bhts,bthd->bshd", probability_low, grad_out)
    grad_pairs = round_low(jnp.stack([grad_keys, grad_values], axis=3)).reshape(BATCH, SRC, HEADS * 2 * HD)
    source_part = jnp.einsum("bsc,dc->bsd", grad_pairs, w_layer.astype(jnp.float32))
    return out_layer, grad_query.reshape(BATCH, TQ, GROUPS, HEAD_COLS), source_part


def reference(encoder_states, w_kv, queries, cotangent, src_len, tgt_len):
    def layer_step(grad_carry, layer_args):
        w_layer, query_layer, cot_layer = layer_args
        out_layer, grad_query, source_part = layer_grads(encoder_states, w_layer, query_layer, cot_layer, src_len, tgt_len)
        return grad_carry + source_part, (out_layer, grad_query)

    zero_grads = jnp.zeros((BATCH, SRC, D), jnp.float32)
    grad_source, stacked = lax.scan(layer_step, zero_grads, (w_kv, queries, cotangent))
    return stacked[0], stacked[1], grad_source.astype(jnp.bfloat16)
```

```python
import jax
import jax.numpy as jnp
from jax import lax
from jax.sharding import PartitionSpec as P

masked_score = -1e30


def shifted(x, axis, k):
    size = lax.axis_size(axis)
    return lax.ppermute(x, axis, [(i, (i + k) % size) for i in range(size)])


def gathered(x, axis):
    size, me = lax.axis_size(axis), lax.axis_index(axis)
    full = jnp.zeros((size,) + x.shape, x.dtype)
    for k in range(size):
        block = x if k == 0 else shifted(x, axis, k)
        full = lax.dynamic_update_index_in_dim(full, block, lax.rem(me - k + size, size), 0)
    return full


def merged(stat, axis):
    size = lax.axis_size(axis)
    parts = [stat] + [shifted(stat, axis, k) for k in range(1, size)]
    top = parts[0][0]
    for part in parts[1:]:
        top = jnp.maximum(top, part[0])
    total = sum(jnp.exp(part[0] - top) * part[1] for part in parts)
    inner = sum(jnp.exp(part[0] - top) * part[2] for part in parts)
    return jnp.stack([top, total, inner])


def summed(pick, axis):
    size, me = lax.axis_size(axis), lax.axis_index(axis)
    held = pick(me).astype(jnp.float32)
    for k in range(1, size):
        held = held + shifted(pick(lax.rem(me + k, size)), axis, k).astype(jnp.float32)
    return held.astype(jnp.bfloat16)


def body(encoder_states, w_kv, queries, cotangent, src_len, tgt_len):
    f32, bf16 = jnp.float32, jnp.bfloat16
    sections = lax.axis_size("section")
    shards = lax.axis_size("seq")
    heads = lax.axis_size("head")
    section = lax.axis_index("section")
    seat = lax.axis_index("seq")
    samples, src_rows, model_width = encoder_states.shape
    layers = w_kv.shape[0]
    pair_cols = w_kv.shape[2]
    head_dim = pair_cols // 2
    chunk = src_rows // sections
    groups = queries.shape[3]
    target_rows = queries.shape[2]
    own_rows = target_rows // shards
    width = model_width // (sections * heads)
    score_scale = head_dim ** (-0.5)

    query_live = jnp.arange(target_rows, dtype=jnp.int32)[None, :] < tgt_len[:, None]
    grad_own = jnp.where(query_live[:, :, None, None], cotangent[0], jnp.zeros((), bf16))
    rows_own = jnp.stack([queries[0], grad_own]).transpose(0, 1, 3, 2, 4)
    rows_own = lax.dynamic_slice_in_dim(rows_own, seat * own_rows, own_rows, axis=3)
    rows_all = lax.all_gather(gathered(rows_own, "section"), "seq", axis=4, tiled=True)
    query_all, grad_all = rows_all[:, 0], rows_all[:, 1]

    share = model_width // shards
    share_of = lax.dynamic_slice_in_dim(w_kv, seat * share, share, axis=1)
    weights = []
    for l in range(layers):
        part = gathered(share_of[l], "section")
        weights.append(lax.all_gather(part, "seq", axis=0, tiled=False))

    source = lax.dynamic_slice_in_dim(encoder_states, section * chunk, chunk, axis=1)
    source = source.reshape(samples, chunk, shards, share)
    position = seat * src_rows + section * chunk + jnp.arange(chunk, dtype=jnp.int32)
    key_live = position[None, :] < src_len[:, None]

    keys, values, exps, grads, factors, deltas = [], [], [], [], [], []
    for l in range(layers):
        pair = jnp.einsum(
            "bpqd,qgdc->gbpc", source, weights[l], preferred_element_type=f32
        ).astype(bf16)
        key, value = pair[..., :head_dim], pair[..., head_dim:]
        s = jnp.einsum("bgtd,gbpd->gbtp", query_all[l], key, preferred_element_type=f32) * score_scale
        s = jnp.where(key_live[None, :, None, :], s, masked_score)
        top = jnp.max(s, axis=-1)
        e = jnp.exp(s - top[..., None])
        gp = jnp.einsum("bgtd,gbpd->gbtp", grad_all[l], value, preferred_element_type=f32)
        mine = jnp.stack([top, jnp.sum(e, axis=-1), jnp.sum(e * gp, axis=-1)])
        whole = merged(merged(mine, "seq"), "section")
        factors.append(jnp.exp(top - whole[0]) / whole[1])
        deltas.append(whole[2] / whole[1])
        keys.append(key)
        values.append(value)
        exps.append(e)
        grads.append(gp)

    results, pairs = [], []
    for l in range(layers):
        p = exps[l] * factors[l][..., None]
        low = p.astype(bf16)
        ds = (p * (grads[l] - deltas[l][..., None])).astype(bf16)
        out = jnp.einsum("gbtp,gbpd->gbtd", low, values[l], preferred_element_type=f32)
        dq = score_scale * jnp.einsum("gbtp,gbpd->gbtd", ds, keys[l], preferred_element_type=f32)
        results.append(jnp.stack([out.astype(bf16), dq.astype(bf16)]))
        gk = score_scale * jnp.einsum("gbtp,bgtd->gbpd", ds, query_all[l], preferred_element_type=f32)
        gv = jnp.einsum("gbtp,bgtd->gbpd", low, grad_all[l], preferred_element_type=f32)
        pairs.append(jnp.concatenate([gk, gv], axis=-1).astype(bf16))

    result = jnp.stack(results)
    result = summed(
        lambda i: lax.dynamic_slice_in_dim(result, i * own_rows, own_rows, axis=4), "seq"
    )
    result = summed(lambda i: lax.dynamic_index_in_dim(result, i, 0, keepdims=False), "section")
    result = result.transpose(0, 2, 3, 1, 4)

    source_part = jnp.zeros((samples, src_rows, width), bf16)
    for b in range(samples):
        term = sum(
            jnp.einsum("gpc,qgdc->pqd", pairs[l][:, b], weights[l], preferred_element_type=f32)
            for l in range(layers)
        )
        term = term.astype(bf16).reshape(chunk, model_width)

        def pick(h, term=term):
            return jnp.stack(
                [
                    lax.dynamic_slice_in_dim(term, (s * heads + h) * width, width, axis=1)
                    for s in range(sections)
                ]
            )

        total = summed(pick, "head")
        for k in range(sections):
            block = lax.dynamic_index_in_dim(total, lax.rem(section + k, sections), 0)
            if k:
                block = shifted(block, "section", k)
            owner = lax.rem(section - k + sections, sections)
            source_part = lax.dynamic_update_slice(source_part, block, (b, owner * chunk, 0))
    return result[0][None], result[1][None], source_part


def solution(mesh):
    placed = (
        P(None, "seq", None),
        P(None, None, ("section", "head")),
        P("section", None, None, None, "head"),
        P("section", None, None, None, "head"),
        P(),
        P(),
    )
    return jax.shard_map(
        body,
        mesh=mesh,
        in_specs=placed,
        out_specs=(
            P("section", None, "seq", None, "head"),
            P("section", None, "seq", None, "head"),
            P(None, "seq", ("section", "head")),
        ),
        check_vma=False,
    )
```
